32 devices in a mesh: prow: 4 (over z), pcol: 8 (over y, x, core).
Axes of the slice: x: 2, y: 2, z: 4, core: 2. Of those that a mesh axis runs over, the one named last changes fastest.
Arguments:
- ancestor_inverse: float32 [16, 4, 128, 8, 8, 128], P(None, 'prow', None, None, 'pcol'), as said below
- panel: float32 [4, 16, 4, 128, 256], P(None, None, 'prow'), may hold values from -0.0625 to 0.0625
- pattern: int32 [4, 16, 4], replicated, may hold values 0 or 1
- diag_term: float32 [4, 256, 256], replicated, may hold values from -6 to 6
Outputs:
- block_column: float32 [4, 16, 4, 128, 256], P(None, 'pcol', 'prow')
- diag_block: float32 [4, 256, 256], replicated
The draws below stay inside these ranges and needn't reach their ends.
Inputs may be any that keep to these rules, and one draw needn't show every extreme that they name: `ancestor_inverse`: A equals its transpose.
All inputs are finite; a program needn't handle non-finite values.
Results may differ from the reference program's by a relative error of at most 0.00007.
Values sent between devices are 32-bit elements; how exact they have to be, the bound alone decides.
A program may use at most 128 MiB of HBM per device.

```python
import jax
import jax.numpy as jnp
from jax import lax

BLK = 128
W = 256
S = 4
CBD = 8
GRID_ROWS = 4
GRID_COLS = 8
RBD = 16
ORDER = 8192


def draw_ancestor_inverse(key, part):
    first = jax.random.fold_in(key, 0)
    raw = jax.random.normal(first, (ORDER, ORDER), jnp.float32)
    mirrored = (raw + raw.T) * 0.7071
    return mirrored.reshape(RBD, GRID_ROWS, BLK, CBD, GRID_COLS, BLK)


def with_ends(array, own_key, least, high):
    dims = array.shape
    spot = [jax.random.randint(jax.random.fold_in(own_key, axis), (), 0, dims[axis]) for axis in range(len(dims))]
    array = array.at[tuple(spot)].set(least)
    longest = dims.index(max(dims))
    spot[longest] = (spot[longest] + 1) % dims[longest]
    return array.at[tuple(spot)].set(high)


def block_levels(key, dims, cuts, smallest, top_value):
    loudness = 1.0
    for position, shards_of in cuts:
        steps = jax.random.uniform(jax.random.fold_in(jax.random.fold_in(key, 6), position), (shards_of,), jnp.float32, smallest / len(cuts), top_value / len(cuts))
        loudness = loudness * jnp.repeat(jnp.exp(steps), dims[position] // shards_of).reshape((-1,) + (1,) * (len(dims) - 1 - position))
    return loudness


def noise(rng, shape, spread, reach, cuts=(), kind=jnp.bfloat16):
    drawn = spread * jax.random.normal(rng, shape, jnp.float32)
    if cuts:
        drawn = drawn * block_levels(rng, shape, cuts, -0.22, 0.18)
    return jnp.clip(drawn, -reach, reach).astype(kind)


def setup_inputs(seed: int = 0) -> dict:
    splits = jax.random.split(jax.random.key(seed), 5)
    return {
        "ancestor_inverse": draw_ancestor_inverse(jax.random.fold_in(splits[4], 71), 0),
        "panel": noise(splits[1], (S, RBD, GRID_ROWS, BLK, W), ORDER ** -0.5, 0.0625, ((2, 4),), jnp.float32),
        "pattern": with_ends((jax.random.randint(splits[2], (S, RBD, GRID_ROWS), 0, 2) < 1).astype(jnp.int32), jax.random.fold_in(splits[2], 1), 0, 1),
        "diag_term": noise(splits[3], (S, W, W), 1.0, 6.0, (), jnp.float32),
    }


def reference(ancestor_inverse, panel, pattern, diag_term):
    inverse_matrix = ancestor_inverse.reshape(ORDER, ORDER)
    row_flags = jnp.repeat(pattern.reshape(S, ORDER // BLK), BLK, axis=1).astype(jnp.float32)
    masked = panel.reshape(S, ORDER, W) * row_flags[:, :, None]

    def one_node(inputs):
        node_rows, node_flags = inputs
        product = jnp.dot(inverse_matrix, node_rows, precision=lax.Precision.HIGHEST)
        return -(product * node_flags[:, None])

    column_block = lax.map(one_node, (masked, row_flags))
    diag_block = diag_term - jnp.einsum("sjw,sjv->swv", masked, column_block, precision=lax.Precision.HIGHEST)
    return column_block.reshape(S, RBD, GRID_ROWS, BLK, W), diag_block
```

```python
import functools

import jax
import jax.numpy as jnp
from jax import lax
from jax.experimental import pallas as pl
from jax.experimental.pallas import tpu as pltpu
from jax.sharding import PartitionSpec as P

MESH = pl.DeviceIdType.MESH


def split(x):
    high = x.astype(jnp.bfloat16)
    return high, (x - high.astype(jnp.float32)).astype(jnp.bfloat16)


def tdot(left, right):
    return lax.dot_general(
        left, right, (((0,), (0,)), ((), ())), preferred_element_type=jnp.float32
    )


def kernel(
    grid_rows, grid_cols,
    tile_ref, panel_ref, pattern_ref, diag_ref,
    column_ref, out_ref,
    panel_high, panel_low, tiles, parts, received, cross, slices, sums, whole,
    tile_sem, send_sem, recv_sem, one_send, one_recv, two_send, two_recv, three_send, three_recv,
):
    row = lax.axis_index("prow")
    col = lax.axis_index("pcol")
    nodes, row_blocks, block, width = panel_ref.shape
    col_blocks = parts.shape[0]
    kept = row_blocks // grid_cols
    depth = row_blocks * block

    def turn(step):
        return lax.rem(step + col + 1, col_blocks)

    def fetch(step):
        slot = lax.rem(step, 2)
        return pltpu.make_async_copy(
            tile_ref.at[:, 0, :, turn(step), 0, :], tiles.at[slot], tile_sem.at[slot]
        )

    fetch(0).start()

    def prepare(flat, carry):
        node, b = flat // row_blocks, lax.rem(flat, row_blocks)
        flag = pattern_ref[node, b, row].astype(jnp.float32)
        high, low = split(panel_ref[node, b] * flag)
        panel_high[node, b] = high
        panel_low[node, b] = low
        return carry

    lax.fori_loop(0, nodes * row_blocks, prepare, 0)

    def send_copy(d):
        b = (d * grid_cols + col) // grid_rows
        owner_row, owner_col = lax.rem(col, grid_rows), b // kept
        slot = lax.rem(b, kept) * grid_rows + row
        copy = pltpu.make_async_remote_copy(
            src_ref=parts.at[d], dst_ref=received.at[slot],
            send_sem=send_sem.at[d], recv_sem=recv_sem.at[slot],
            device_id=(owner_row, owner_col), device_id_type=MESH,
        )
        mine = jnp.logical_and(owner_row == row, owner_col == col)
        return copy, mine, slot

    def produce(step, carry):
        d = turn(step)
        slot = lax.rem(step, 2)
        fetch(step).wait()

        @pl.when(step + 1 < col_blocks)
        def _():
            fetch(step + 1).start()

        high, low = split(tiles[slot].reshape(depth, block))
        both = jnp.concatenate([high, low], axis=1)

        def node_product(node, inner):
            upper = panel_high[node].reshape(depth, width)
            lower = panel_low[node].reshape(depth, width)
            double = tdot(both, upper)
            parts[d, node] = double[:block] + double[block:] + tdot(high, lower)
            return inner

        lax.fori_loop(0, nodes, node_product, 0)
        copy, mine, place = send_copy(d)

        @pl.when(jnp.logical_not(mine))
        def _():
            copy.start()

        @pl.when(mine)
        def _():
            received[place] = parts[d]

        return carry

    lax.fori_loop(0, col_blocks, produce, 0)

    def arrive(slot, carry):
        b = col * kept + slot // grid_rows
        source_col = lax.rem(b * grid_rows + row, grid_cols)
        source_row = lax.rem(slot, grid_rows)

        @pl.when(jnp.logical_not(jnp.logical_and(source_col == col, source_row == row)))
        def _():
            pltpu.make_async_remote_copy(
                src_ref=parts.at[0], dst_ref=received.at[slot],
                send_sem=send_sem.at[0], recv_sem=recv_sem.at[slot],
                device_id=(source_row, source_col), device_id_type=MESH,
            ).wait_recv()

        return carry

    lax.fori_loop(0, kept * grid_rows, arrive, 0)

    def close(node, carry):
        total = None
        for k in range(kept):
            b = col * kept + k
            value = received[k * grid_rows, node]
            for source in range(1, grid_rows):
                value = value + received[k * grid_rows + source, node]
            flag = pattern_ref[node, b, row].astype(jnp.float32)
            value = -(value * flag)
            column_ref[node, k] = value
            high, low = split(value)
            left_high, left_low = panel_high[node, b], panel_low[node, b]
            term = tdot(left_high, high) + tdot(left_high, low) + tdot(left_low, high)
            total = term if total is None else total + term
        cross[pl.ds(node * width, width), :] = total
        return carry

    lax.fori_loop(0, nodes, close, 0)

    share = nodes * width // grid_cols

    def piece(index):
        return pl.ds(pl.multiple_of(index * share, 8), share)

    def one(j):
        target = lax.rem(col + j, grid_cols)
        return pltpu.make_async_remote_copy(
            src_ref=cross.at[piece(target)], dst_ref=slices.at[j],
            send_sem=one_send.at[j], recv_sem=one_recv.at[j],
            device_id=(row, target), device_id_type=MESH,
        )

    def two(j):
        target = lax.rem(row + j, grid_rows)
        return pltpu.make_async_remote_copy(
            src_ref=sums.at[row], dst_ref=sums.at[row],
            send_sem=two_send.at[j], recv_sem=two_recv.at[j],
            device_id=(target, col), device_id_type=MESH,
        )

    def two_arrival(j):
        source = lax.rem(row - j + grid_rows, grid_rows)
        return pltpu.make_async_remote_copy(
            src_ref=sums.at[source], dst_ref=sums.at[source],
            send_sem=two_send.at[j], recv_sem=two_recv.at[j],
            device_id=(source, col), device_id_type=MESH,
        )

    def three(j):
        target = lax.rem(col + j, grid_cols)
        return pltpu.make_async_remote_copy(
            src_ref=whole.at[piece(col)], dst_ref=whole.at[piece(col)],
            send_sem=three_send.at[j], recv_sem=three_recv.at[j],
            device_id=(row, target), device_id_type=MESH,
        )

    def three_arrival(j):
        source = lax.rem(col - j + grid_cols, grid_cols)
        return pltpu.make_async_remote_copy(
            src_ref=whole.at[piece(source)], dst_ref=whole.at[piece(source)],
            send_sem=three_send.at[j], recv_sem=three_recv.at[j],
            device_id=(row, source), device_id_type=MESH,
        )

    def each(count, action):
        def body(j, carry):
            action(j)
            return carry

        lax.fori_loop(1, count, body, 0)

    each(grid_cols, lambda j: one(j).start())
    each(grid_cols, lambda j: one(j).wait_recv())
    value = cross[piece(col), :]
    for j in range(1, grid_cols):
        value = value + slices[j]
    sums[row] = value
    each(grid_rows, lambda j: two(j).start())
    each(grid_rows, lambda j: two_arrival(j).wait_recv())
    value = sums[0]
    for j in range(1, grid_rows):
        value = value + sums[j]
    whole[piece(col), :] = diag_ref[piece(col), :] - value
    each(grid_cols, lambda j: three(j).start())
    each(grid_cols, lambda j: three_arrival(j).wait_recv())
    out_ref[...] = whole[...]
    each(grid_cols, lambda j: one(j).wait_send())
    each(grid_rows, lambda j: two(j).wait_send())
    each(grid_cols, lambda j: three(j).wait_send())

    def leave(d, carry):
        copy, mine, _ = send_copy(d)

        @pl.when(jnp.logical_not(mine))
        def _():
            copy.wait_send()

        return carry

    lax.fori_loop(0, col_blocks, leave, 0)


def local(ancestor_inverse, panel, pattern, diag_term):
    grid_rows = lax.axis_size("prow")
    grid_cols = lax.axis_size("pcol")
    nodes, row_blocks, _, block, width = panel.shape
    col_blocks = ancestor_inverse.shape[3]
    kept = row_blocks // grid_cols
    f32 = jnp.float32
    share = nodes * width // grid_cols
    dma = pltpu.SemaphoreType.DMA
    vmem = pl.BlockSpec(memory_space=pltpu.VMEM)
    column, diag = pl.pallas_call(
        functools.partial(kernel, grid_rows, grid_cols),
        out_shape=(
            jax.ShapeDtypeStruct((nodes, kept, block, width), f32),
            jax.ShapeDtypeStruct((nodes * width, width), f32),
        ),
        in_specs=[
            pl.BlockSpec(memory_space=pl.ANY),
            vmem,
            pl.BlockSpec(memory_space=pltpu.SMEM),
            vmem,
        ],
        out_specs=(vmem, vmem),
        scratch_shapes=[
            pltpu.VMEM((nodes, row_blocks, block, width), jnp.bfloat16),
            pltpu.VMEM((nodes, row_blocks, block, width), jnp.bfloat16),
            pltpu.VMEM((2, row_blocks, block, block), f32),
            pltpu.VMEM((col_blocks, nodes, block, width), f32),
            pltpu.VMEM((kept * grid_rows, nodes, block, width), f32),
            pltpu.VMEM((nodes * width, width), f32),
            pltpu.VMEM((grid_cols, share, width), f32),
            pltpu.VMEM((grid_rows, share, width), f32),
            pltpu.VMEM((nodes * width, width), f32),
            dma((2,)),
            dma((col_blocks,)),
            dma((kept * grid_rows,)),
            dma((grid_cols,)),
            dma((grid_cols,)),
            dma((grid_rows,)),
            dma((grid_rows,)),
            dma((grid_cols,)),
            dma((grid_cols,)),
        ],
        compiler_params=pltpu.CompilerParams(
            has_side_effects=True, vmem_limit_bytes=52 * 1024 * 1024
        ),
    )(
        ancestor_inverse,
        panel.reshape(nodes, row_blocks, block, width),
        pattern,
        diag_term.reshape(nodes * width, width),
    )
    return column[:, :, None], diag.reshape(nodes, width, width)


def solution(mesh):
    in_specs = (
        P(None, "prow", None, None, "pcol", None),
        P(None, None, "prow", None, None),
        P(),
        P(),
    )
    out_specs = (P(None, "pcol", "prow", None, None), P())
    return jax.shard_map(local, mesh=mesh, in_specs=in_specs, out_specs=out_specs, check_vma=False)
```

```python
import functools

import jax
import jax.numpy as jnp
from jax import lax
from jax.experimental import pallas as pl
from jax.experimental.pallas import tpu as pltpu
from jax.sharding import PartitionSpec as P

MESH = pl.DeviceIdType.MESH


def split(x):
    high = x.astype(jnp.bfloat16)
    return high, (x - high.astype(jnp.float32)).astype(jnp.bfloat16)


def tdot(left, right):
    return lax.dot_general(
        left, right, (((0,), (0,)), ((), ())), preferred_element_type=jnp.float32
    )


def kernel(
    grid_rows, grid_cols,
    tile_ref, panel_ref, pattern_ref, diag_ref,
    column_ref, out_ref,
    panel_high, panel_low, tiles, parts, received, inbox, cross, slices, sums, whole,
    tile_sem, send_sem, recv_sem, hop_send, hop_recv, one_send, one_recv, two_send, two_recv, three_send, three_recv,
):
    row = lax.axis_index("prow")
    col = lax.axis_index("pcol")
    nodes, row_blocks, block, width = panel_ref.shape
    col_blocks = parts.shape[0]
    kept = row_blocks // grid_cols
    depth = row_blocks * block

    def turn(step):
        return lax.rem(step + col + 1, col_blocks)

    def fetch(step):
        slot = lax.rem(step, 2)
        return pltpu.make_async_copy(
            tile_ref.at[:, 0, :, turn(step), 0, :], tiles.at[slot], tile_sem.at[slot]
        )

    fetch(0).start()

    def prepare(flat, carry):
        node, b = flat // row_blocks, lax.rem(flat, row_blocks)
        flag = pattern_ref[node, b, row].astype(jnp.float32)
        high, low = split(panel_ref[node, b] * flag)
        panel_high[node, b] = high
        panel_low[node, b] = low
        return carry

    lax.fori_loop(0, nodes * row_blocks, prepare, 0)

    def send_copy(d):
        b = (d * grid_cols + col) // grid_rows
        owner_col = b // kept
        slot = lax.rem(b, kept) * grid_rows + lax.rem(col, grid_rows)
        copy = pltpu.make_async_remote_copy(
            src_ref=parts.at[d], dst_ref=received.at[slot],
            send_sem=send_sem.at[d], recv_sem=recv_sem.at[slot],
            device_id=(row, owner_col), device_id_type=MESH,
        )
        return copy, owner_col == col, slot

    def produce(step, carry):
        d = turn(step)
        slot = lax.rem(step, 2)
        fetch(step).wait()

        @pl.when(step + 1 < col_blocks)
        def _():
            fetch(step + 1).start()

        high, low = split(tiles[slot].reshape(depth, block))
        both = jnp.concatenate([high, low], axis=1)

        def node_product(node, inner):
            upper = panel_high[node].reshape(depth, width)
            lower = panel_low[node].reshape(depth, width)
            double = tdot(both, upper)
            parts[d, node] = double[:block] + double[block:] + tdot(high, lower)
            return inner

        lax.fori_loop(0, nodes, node_product, 0)
        copy, mine, place = send_copy(d)

        @pl.when(jnp.logical_not(mine))
        def _():
            copy.start()

        @pl.when(mine)
        def _():
            received[place] = parts[d]

        return carry

    lax.fori_loop(0, col_blocks, produce, 0)

    slots = kept * grid_rows

    def hop(slot, side, target_row):
        return pltpu.make_async_remote_copy(
            src_ref=received.at[slot], dst_ref=inbox.at[side * slots + slot],
            send_sem=hop_send.at[slot], recv_sem=hop_recv.at[side * slots + slot],
            device_id=(target_row, col), device_id_type=MESH,
        )

    def absorb(slot, side, source_row):
        hop(slot, side, source_row).wait_recv()

        def add(node, carry):
            received[slot, node] += inbox[side * slots + slot, node]
            return carry

        lax.fori_loop(0, nodes, add, 0)

    def relay(index, carry):
        turn_of, k = index // kept, lax.rem(index, kept)
        half, low_end = turn_of // 2, lax.rem(turn_of, 2)
        target = low_end * half + (1 - low_end) * (grid_rows - 1 - half)
        slot = k * grid_rows + target
        source_col = lax.rem((col * kept + k) * grid_rows + target, grid_cols)

        @pl.when(source_col != col)
        def _():
            pltpu.make_async_remote_copy(
                src_ref=parts.at[0], dst_ref=received.at[slot],
                send_sem=send_sem.at[0], recv_sem=recv_sem.at[slot],
                device_id=(row, source_col), device_id_type=MESH,
            ).wait_recv()

        @pl.when(row < target)
        def _():
            @pl.when(row > 0)
            def _():
                absorb(slot, 0, row - 1)

            hop(slot, 0, row + 1).start()

        @pl.when(row > target)
        def _():
            @pl.when(row < grid_rows - 1)
            def _():
                absorb(slot, 1, row + 1)

            hop(slot, 1, row - 1).start()

        return carry

    lax.fori_loop(0, slots, relay, 0)

    def settle(k, carry):
        slot = k * grid_rows + row

        @pl.when(row > 0)
        def _():
            absorb(slot, 0, row - 1)

        @pl.when(row < grid_rows - 1)
        def _():
            absorb(slot, 1, row + 1)

        return carry

    lax.fori_loop(0, kept, settle, 0)

    def close(node, carry):
        total = None
        for k in range(kept):
            b = col * kept + k
            value = received[k * grid_rows + row, node]
            flag = pattern_ref[node, b, row].astype(jnp.float32)
            value = -(value * flag)
            column_ref[node, k] = value
            high, low = split(value)
            left_high, left_low = panel_high[node, b], panel_low[node, b]
            term = tdot(left_high, high) + tdot(left_high, low) + tdot(left_low, high)
            total = term if total is None else total + term
        cross[pl.ds(node * width, width), :] = total
        return carry

    lax.fori_loop(0, nodes, close, 0)

    share = nodes * width // grid_cols

    def piece(index):
        return pl.ds(pl.multiple_of(index * share, 8), share)

    def one(j):
        target = lax.rem(col + j, grid_cols)
        return pltpu.make_async_remote_copy(
            src_ref=cross.at[piece(target)], dst_ref=slices.at[j],
            send_sem=one_send.at[j], recv_sem=one_recv.at[j],
            device_id=(row, target), device_id_type=MESH,
        )

    def two(j):
        target = lax.rem(row + j, grid_rows)
        return pltpu.make_async_remote_copy(
            src_ref=sums.at[row], dst_ref=sums.at[row],
            send_sem=two_send.at[j], recv_sem=two_recv.at[j],
            device_id=(target, col), device_id_type=MESH,
        )

    def two_arrival(j):
        source = lax.rem(row - j + grid_rows, grid_rows)
        return pltpu.make_async_remote_copy(
            src_ref=sums.at[source], dst_ref=sums.at[source],
            send_sem=two_send.at[j], recv_sem=two_recv.at[j],
            device_id=(source, col), device_id_type=MESH,
        )

    def three(j):
        target = lax.rem(col + j, grid_cols)
        return pltpu.make_async_remote_copy(
            src_ref=whole.at[piece(col)], dst_ref=whole.at[piece(col)],
            send_sem=three_send.at[j], recv_sem=three_recv.at[j],
            device_id=(row, target), device_id_type=MESH,
        )

    def three_arrival(j):
        source = lax.rem(col - j + grid_cols, grid_cols)
        return pltpu.make_async_remote_copy(
            src_ref=whole.at[piece(source)], dst_ref=whole.at[piece(source)],
            send_sem=three_send.at[j], recv_sem=three_recv.at[j],
            device_id=(row, source), device_id_type=MESH,
        )

    def each(count, action):
        def body(j, carry):
            action(j)
            return carry

        lax.fori_loop(1, count, body, 0)

    each(grid_cols, lambda j: one(j).start())
    each(grid_cols, lambda j: one(j).wait_recv())
    value = cross[piece(col), :]
    for j in range(1, grid_cols):
        value = value + slices[j]
    sums[row] = value
    each(grid_rows, lambda j: two(j).start())
    each(grid_rows, lambda j: two_arrival(j).wait_recv())
    value = sums[0]
    for j in range(1, grid_rows):
        value = value + sums[j]
    whole[piece(col), :] = diag_ref[piece(col), :] - value
    each(grid_cols, lambda j: three(j).start())
    each(grid_cols, lambda j: three_arrival(j).wait_recv())
    out_ref[...] = whole[...]
    each(grid_cols, lambda j: one(j).wait_send())
    each(grid_rows, lambda j: two(j).wait_send())
    each(grid_cols, lambda j: three(j).wait_send())

    def leave(d, carry):
        copy, mine, _ = send_copy(d)

        @pl.when(jnp.logical_not(mine))
        def _():
            copy.wait_send()

        return carry

    lax.fori_loop(0, col_blocks, leave, 0)

    def leave_hop(slot, carry):
        target = lax.rem(slot, grid_rows)

        @pl.when(row < target)
        def _():
            hop(slot, 0, row + 1).wait_send()

        @pl.when(row > target)
        def _():
            hop(slot, 1, row - 1).wait_send()

        return carry

    lax.fori_loop(0, slots, leave_hop, 0)


def local(ancestor_inverse, panel, pattern, diag_term):
    grid_rows = lax.axis_size("prow")
    grid_cols = lax.axis_size("pcol")
    nodes, row_blocks, _, block, width = panel.shape
    col_blocks = ancestor_inverse.shape[3]
    kept = row_blocks // grid_cols
    f32 = jnp.float32
    share = nodes * width // grid_cols
    dma = pltpu.SemaphoreType.DMA
    vmem = pl.BlockSpec(memory_space=pltpu.VMEM)
    column, diag = pl.pallas_call(
        functools.partial(kernel, grid_rows, grid_cols),
        out_shape=(
            jax.ShapeDtypeStruct((nodes, kept, block, width), f32),
            jax.ShapeDtypeStruct((nodes * width, width), f32),
        ),
        in_specs=[
            pl.BlockSpec(memory_space=pl.ANY),
            vmem,
            pl.BlockSpec(memory_space=pltpu.SMEM),
            vmem,
        ],
        out_specs=(vmem, vmem),
        scratch_shapes=[
            pltpu.VMEM((nodes, row_blocks, block, width), jnp.bfloat16),
            pltpu.VMEM((nodes, row_blocks, block, width), jnp.bfloat16),
            pltpu.VMEM((2, row_blocks, block, block), f32),
            pltpu.VMEM((col_blocks, nodes, block, width), f32),
            pltpu.VMEM((kept * grid_rows, nodes, block, width), f32),
            pltpu.VMEM((2 * kept * grid_rows, nodes, block, width), f32),
            pltpu.VMEM((nodes * width, width), f32),
            pltpu.VMEM((grid_cols, share, width), f32),
            pltpu.VMEM((grid_rows, share, width), f32),
            pltpu.VMEM((nodes * width, width), f32),
            dma((2,)),
            dma((col_blocks,)),
            dma((kept * grid_rows,)),
            dma((kept * grid_rows,)),
            dma((2 * kept * grid_rows,)),
            dma((grid_cols,)),
            dma((grid_cols,)),
            dma((grid_rows,)),
            dma((grid_rows,)),
            dma((grid_cols,)),
            dma((grid_cols,)),
        ],
        compiler_params=pltpu.CompilerParams(
            has_side_effects=True, vmem_limit_bytes=52 * 1024 * 1024
        ),
    )(
        ancestor_inverse,
        panel.reshape(nodes, row_blocks, block, width),
        pattern,
        diag_term.reshape(nodes * width, width),
    )
    return column[:, :, None], diag.reshape(nodes, width, width)


def solution(mesh):
    in_specs = (
        P(None, "prow", None, None, "pcol", None),
        P(None, None, "prow", None, None),
        P(),
        P(),
    )
    out_specs = (P(None, "pcol", "prow", None, None), P())
    return jax.shard_map(local, mesh=mesh, in_specs=in_specs, out_specs=out_specs, check_vma=False)
```

```python
import functools

import jax
import jax.numpy as jnp
from jax import lax
from jax.experimental import pallas as pl
from jax.experimental.pallas import tpu as pltpu
from jax.sharding import PartitionSpec as P

MESH = pl.DeviceIdType.MESH


def split(x):
    high = x.astype(jnp.bfloat16)
    return high, (x - high.astype(jnp.float32)).astype(jnp.bfloat16)


def tdot(left, right):
    return lax.dot_general(
        left, right, (((0,), (0,)), ((), ())), preferred_element_type=jnp.float32
    )


def kernel(
    grid_rows, grid_cols,
    tile_ref, panel_ref, pattern_ref, diag_ref,
    column_ref, out_ref,
    panel_high, panel_low, tiles, parts, received, inbox, cross, slices, sums, whole,
    tile_sem, send_sem, recv_sem, hop_send, hop_recv, one_send, one_recv, two_send, two_recv, three_send, three_recv,
):
    row = lax.axis_index("prow")
    col = lax.axis_index("pcol")
    nodes, row_blocks, block, width = panel_ref.shape
    col_blocks = parts.shape[0]
    kept = row_blocks // grid_cols
    depth = row_blocks * block

    def turn(step):
        return lax.rem(step + col + 1, col_blocks)

    def fetch(step):
        slot = lax.rem(step, 2)
        return pltpu.make_async_copy(
            tile_ref.at[:, 0, :, turn(step), 0, :], tiles.at[slot], tile_sem.at[slot]
        )

    fetch(0).start()

    def prepare(flat, carry):
        node, b = flat // row_blocks, lax.rem(flat, row_blocks)
        flag = pattern_ref[node, b, row].astype(jnp.float32)
        high, low = split(panel_ref[node, b] * flag)
        panel_high[node, b] = high
        panel_low[node, b] = low
        return carry

    lax.fori_loop(0, nodes * row_blocks, prepare, 0)

    def send_copy(d):
        b = (d * grid_cols + col) // grid_rows
        owner_col = b // kept
        slot = lax.rem(b, kept) * grid_rows + lax.rem(col, grid_rows)
        copy = pltpu.make_async_remote_copy(
            src_ref=parts.at[d], dst_ref=received.at[slot],
            send_sem=send_sem.at[d], recv_sem=recv_sem.at[slot],
            device_id=(row, owner_col), device_id_type=MESH,
        )
        return copy, owner_col == col, slot

    slots = kept * grid_rows
    lag = 2

    def hop(slot, side, target_row):
        return pltpu.make_async_remote_copy(
            src_ref=received.at[slot], dst_ref=inbox.at[side * slots + slot],
            send_sem=hop_send.at[slot], recv_sem=hop_recv.at[side * slots + slot],
            device_id=(target_row, col), device_id_type=MESH,
        )

    def absorb(slot, side, source_row):
        hop(slot, side, source_row).wait_recv()

        def add(node, carry):
            received[slot, node] += inbox[side * slots + slot, node]
            return carry

        lax.fori_loop(0, nodes, add, 0)

    def relay(index, carry):
        first = (col * col_blocks) // grid_cols
        slot = lax.rem(first - 1 - index + 2 * col_blocks, col_blocks)
        k, target = slot // grid_rows, lax.rem(slot, grid_rows)
        source_col = lax.rem((col * kept + k) * grid_rows + target, grid_cols)

        @pl.when(source_col != col)
        def _():
            pltpu.make_async_remote_copy(
                src_ref=parts.at[0], dst_ref=received.at[slot],
                send_sem=send_sem.at[0], recv_sem=recv_sem.at[slot],
                device_id=(row, source_col), device_id_type=MESH,
            ).wait_recv()

        @pl.when(row < target)
        def _():
            @pl.when(row > 0)
            def _():
                absorb(slot, 0, row - 1)

            hop(slot, 0, row + 1).start()

        @pl.when(row > target)
        def _():
            @pl.when(row < grid_rows - 1)
            def _():
                absorb(slot, 1, row + 1)

            hop(slot, 1, row - 1).start()

        return carry

    def produce(step, carry):
        d = turn(step)
        slot = lax.rem(step, 2)
        fetch(step).wait()

        @pl.when(step + 1 < col_blocks)
        def _():
            fetch(step + 1).start()

        high, low = split(tiles[slot].reshape(depth, block))
        both = jnp.concatenate([high, low], axis=1)

        def node_product(node, inner):
            upper = panel_high[node].reshape(depth, width)
            lower = panel_low[node].reshape(depth, width)
            double = tdot(both, upper)
            parts[d, node] = double[:block] + double[block:] + tdot(high, lower)
            return inner

        lax.fori_loop(0, nodes, node_product, 0)
        copy, mine, place = send_copy(d)

        @pl.when(jnp.logical_not(mine))
        def _():
            copy.start()

        @pl.when(mine)
        def _():
            received[place] = parts[d]

        @pl.when(step >= lag)
        def _():
            relay(step - lag, 0)

        return carry

    lax.fori_loop(0, col_blocks, produce, 0)

    lax.fori_loop(slots - lag, slots, relay, 0)

    def settle(k, carry):
        slot = k * grid_rows + row

        @pl.when(row > 0)
        def _():
            absorb(slot, 0, row - 1)

        @pl.when(row < grid_rows - 1)
        def _():
            absorb(slot, 1, row + 1)

        return carry

    lax.fori_loop(0, kept, settle, 0)

    def close(node, carry):
        total = None
        for k in range(kept):
            b = col * kept + k
            value = received[k * grid_rows + row, node]
            flag = pattern_ref[node, b, row].astype(jnp.float32)
            value = -(value * flag)
            column_ref[node, k] = value
            high, low = split(value)
            left_high, left_low = panel_high[node, b], panel_low[node, b]
            term = tdot(left_high, high) + tdot(left_high, low) + tdot(left_low, high)
            total = term if total is None else total + term
        cross[pl.ds(node * width, width), :] = total
        return carry

    lax.fori_loop(0, nodes, close, 0)

    share = nodes * width // grid_cols

    def piece(index):
        return pl.ds(pl.multiple_of(index * share, 8), share)

    def one(j):
        target = lax.rem(col + j, grid_cols)
        return pltpu.make_async_remote_copy(
            src_ref=cross.at[piece(target)], dst_ref=slices.at[j],
            send_sem=one_send.at[j], recv_sem=one_recv.at[j],
            device_id=(row, target), device_id_type=MESH,
        )

    def two(j):
        target = lax.rem(row + j, grid_rows)
        return pltpu.make_async_remote_copy(
            src_ref=sums.at[row], dst_ref=sums.at[row],
            send_sem=two_send.at[j], recv_sem=two_recv.at[j],
            device_id=(target, col), device_id_type=MESH,
        )

    def two_arrival(j):
        source = lax.rem(row - j + grid_rows, grid_rows)
        return pltpu.make_async_remote_copy(
            src_ref=sums.at[source], dst_ref=sums.at[source],
            send_sem=two_send.at[j], recv_sem=two_recv.at[j],
            device_id=(source, col), device_id_type=MESH,
        )

    def three(j):
        target = lax.rem(col + j, grid_cols)
        return pltpu.make_async_remote_copy(
            src_ref=whole.at[piece(col)], dst_ref=whole.at[piece(col)],
            send_sem=three_send.at[j], recv_sem=three_recv.at[j],
            device_id=(row, target), device_id_type=MESH,
        )

    def three_arrival(j):
        source = lax.rem(col - j + grid_cols, grid_cols)
        return pltpu.make_async_remote_copy(
            src_ref=whole.at[piece(source)], dst_ref=whole.at[piece(source)],
            send_sem=three_send.at[j], recv_sem=three_recv.at[j],
            device_id=(row, source), device_id_type=MESH,
        )

    def each(count, action):
        def body(j, carry):
            action(j)
            return carry

        lax.fori_loop(1, count, body, 0)

    each(grid_cols, lambda j: one(j).start())
    each(grid_cols, lambda j: one(j).wait_recv())
    value = cross[piece(col), :]
    for j in range(1, grid_cols):
        value = value + slices[j]
    sums[row] = value
    each(grid_rows, lambda j: two(j).start())
    each(grid_rows, lambda j: two_arrival(j).wait_recv())
    value = sums[0]
    for j in range(1, grid_rows):
        value = value + sums[j]
    whole[piece(col), :] = diag_ref[piece(col), :] - value
    each(grid_cols, lambda j: three(j).start())
    each(grid_cols, lambda j: three_arrival(j).wait_recv())
    out_ref[...] = whole[...]
    each(grid_cols, lambda j: one(j).wait_send())
    each(grid_rows, lambda j: two(j).wait_send())
    each(grid_cols, lambda j: three(j).wait_send())

    def leave(d, carry):
        copy, mine, _ = send_copy(d)

        @pl.when(jnp.logical_not(mine))
        def _():
            copy.wait_send()

        return carry

    lax.fori_loop(0, col_blocks, leave, 0)

    def leave_hop(slot, carry):
        target = lax.rem(slot, grid_rows)

        @pl.when(row < target)
        def _():
            hop(slot, 0, row + 1).wait_send()

        @pl.when(row > target)
        def _():
            hop(slot, 1, row - 1).wait_send()

        return carry

    lax.fori_loop(0, slots, leave_hop, 0)


def local(ancestor_inverse, panel, pattern, diag_term):
    grid_rows = lax.axis_size("prow")
    grid_cols = lax.axis_size("pcol")
    nodes, row_blocks, _, block, width = panel.shape
    col_blocks = ancestor_inverse.shape[3]
    kept = row_blocks // grid_cols
    f32 = jnp.float32
    share = nodes * width // grid_cols
    dma = pltpu.SemaphoreType.DMA
    vmem = pl.BlockSpec(memory_space=pltpu.VMEM)
    column, diag = pl.pallas_call(
        functools.partial(kernel, grid_rows, grid_cols),
        out_shape=(
            jax.ShapeDtypeStruct((nodes, kept, block, width), f32),
            jax.ShapeDtypeStruct((nodes * width, width), f32),
        ),
        in_specs=[
            pl.BlockSpec(memory_space=pl.ANY),
            vmem,
            pl.BlockSpec(memory_space=pltpu.SMEM),
            vmem,
        ],
        out_specs=(vmem, vmem),
        scratch_shapes=[
            pltpu.VMEM((nodes, row_blocks, block, width), jnp.bfloat16),
            pltpu.VMEM((nodes, row_blocks, block, width), jnp.bfloat16),
            pltpu.VMEM((2, row_blocks, block, block), f32),
            pltpu.VMEM((col_blocks, nodes, block, width), f32),
            pltpu.VMEM((kept * grid_rows, nodes, block, width), f32),
            pltpu.VMEM((2 * kept * grid_rows, nodes, block, width), f32),
            pltpu.VMEM((nodes * width, width), f32),
            pltpu.VMEM((grid_cols, share, width), f32),
            pltpu.VMEM((grid_rows, share, width), f32),
            pltpu.VMEM((nodes * width, width), f32),
            dma((2,)),
            dma((col_blocks,)),
            dma((kept * grid_rows,)),
            dma((kept * grid_rows,)),
            dma((2 * kept * grid_rows,)),
            dma((grid_cols,)),
            dma((grid_cols,)),
            dma((grid_rows,)),
            dma((grid_rows,)),
            dma((grid_cols,)),
            dma((grid_cols,)),
        ],
        compiler_params=pltpu.CompilerParams(
            has_side_effects=True, vmem_limit_bytes=52 * 1024 * 1024
        ),
    )(
        ancestor_inverse,
        panel.reshape(nodes, row_blocks, block, width),
        pattern,
        diag_term.reshape(nodes * width, width),
    )
    return column[:, :, None], diag.reshape(nodes, width, width)


def solution(mesh):
    in_specs = (
        P(None, "prow", None, None, "pcol", None),
        P(None, None, "prow", None, None),
        P(),
        P(),
    )
    out_specs = (P(None, "pcol", "prow", None, None), P())
    return jax.shard_map(local, mesh=mesh, in_specs=in_specs, out_specs=out_specs, check_vma=False)
```

```python
import functools

import jax
import jax.numpy as jnp
from jax import lax
from jax.experimental import pallas as pl
from jax.experimental.pallas import tpu as pltpu
from jax.sharding import PartitionSpec as P

MESH = pl.DeviceIdType.MESH


def split(x):
    high = x.astype(jnp.bfloat16)
    return high, (x - high.astype(jnp.float32)).astype(jnp.bfloat16)


def tdot(left, right):
    return lax.dot_general(
        left, right, (((0,), (0,)), ((), ())), preferred_element_type=jnp.float32
    )


def kernel(
    grid_rows, grid_cols,
    tile_ref, panel_ref, pattern_ref, diag_ref,
    column_ref, out_ref,
    panel_high, panel_low, tiles, parts, received, inbox, cross, slices, sums, whole,
    tile_sem, send_sem, recv_sem, hop_send, hop_recv, one_send, one_recv, two_send, two_recv, three_send, three_recv,
):
    row = lax.axis_index("prow")
    col = lax.axis_index("pcol")
    nodes, row_blocks, block, width = panel_ref.shape
    col_blocks = parts.shape[0]
    kept = row_blocks // grid_cols
    depth = row_blocks * block

    def turn(step):
        return lax.rem(step + col + 1, col_blocks)

    def fetch(step):
        slot = lax.rem(step, 2)
        return pltpu.make_async_copy(
            tile_ref.at[:, 0, :, turn(step), 0, :], tiles.at[slot], tile_sem.at[slot]
        )

    fetch(0).start()

    def prepare(flat, carry):
        node, b = flat // row_blocks, lax.rem(flat, row_blocks)
        flag = pattern_ref[node, b, row].astype(jnp.float32)
        high, low = split(panel_ref[node, b] * flag)
        panel_high[node, b] = high
        panel_low[node, b] = low
        return carry

    lax.fori_loop(0, nodes * row_blocks, prepare, 0)

    def send_copy(d):
        b = (d * grid_cols + col) // grid_rows
        owner_col = b // kept
        slot = lax.rem(b, kept) * grid_rows + lax.rem(col, grid_rows)
        copy = pltpu.make_async_remote_copy(
            src_ref=parts.at[d], dst_ref=received.at[slot],
            send_sem=send_sem.at[d], recv_sem=recv_sem.at[slot],
            device_id=(row, owner_col), device_id_type=MESH,
        )
        return copy, owner_col == col, slot

    slots = kept * grid_rows
    lag = 2

    def hop(slot, side, target_row):
        return pltpu.make_async_remote_copy(
            src_ref=received.at[slot], dst_ref=inbox.at[side * slots + slot],
            send_sem=hop_send.at[slot], recv_sem=hop_recv.at[side * slots + slot],
            device_id=(target_row, col), device_id_type=MESH,
        )

    def absorb(slot, side, source_row):
        hop(slot, side, source_row).wait_recv()

        def add(node, carry):
            received[slot, node] += inbox[side * slots + slot, node]
            return carry

        lax.fori_loop(0, nodes, add, 0)

    def relay(index, carry):
        first = (col * col_blocks) // grid_cols
        slot = lax.rem(first - 1 - index + 2 * col_blocks, col_blocks)
        k, target = slot // grid_rows, lax.rem(slot, grid_rows)
        source_col = lax.rem((col * kept + k) * grid_rows + target, grid_cols)

        @pl.when(source_col != col)
        def _():
            pltpu.make_async_remote_copy(
                src_ref=parts.at[0], dst_ref=received.at[slot],
                send_sem=send_sem.at[0], recv_sem=recv_sem.at[slot],
                device_id=(row, source_col), device_id_type=MESH,
            ).wait_recv()

        @pl.when(row < target)
        def _():
            @pl.when(row > 0)
            def _():
                absorb(slot, 0, row - 1)

            hop(slot, 0, row + 1).start()

        @pl.when(row > target)
        def _():
            @pl.when(row < grid_rows - 1)
            def _():
                absorb(slot, 1, row + 1)

            hop(slot, 1, row - 1).start()

        return carry

    def produce(step, carry):
        d = turn(step)
        slot = lax.rem(step, 2)
        fetch(step).wait()

        @pl.when(step + 1 < col_blocks)
        def _():
            fetch(step + 1).start()

        high, low = split(tiles[slot].reshape(depth, block).T)
        both = jnp.concatenate([high, low], axis=0)

        def node_product(node, inner):
            upper = panel_high[node].reshape(depth, width)
            lower = panel_low[node].reshape(depth, width)
            double = jnp.dot(both, upper, preferred_element_type=jnp.float32)
            parts[d, node] = double[:block] + double[block:] + jnp.dot(
                high, lower, preferred_element_type=jnp.float32
            )
            return inner

        lax.fori_loop(0, nodes, node_product, 0)
        copy, mine, place = send_copy(d)

        @pl.when(jnp.logical_not(mine))
        def _():
            copy.start()

        @pl.when(mine)
        def _():
            received[place] = parts[d]

        @pl.when(step >= lag)
        def _():
            relay(step - lag, 0)

        return carry

    lax.fori_loop(0, col_blocks, produce, 0)

    lax.fori_loop(slots - lag, slots, relay, 0)

    def settle(k, carry):
        slot = k * grid_rows + row

        @pl.when(row > 0)
        def _():
            absorb(slot, 0, row - 1)

        @pl.when(row < grid_rows - 1)
        def _():
            absorb(slot, 1, row + 1)

        return carry

    lax.fori_loop(0, kept, settle, 0)

    def close(node, carry):
        total = None
        for k in range(kept):
            b = col * kept + k
            value = received[k * grid_rows + row, node]
            flag = pattern_ref[node, b, row].astype(jnp.float32)
            value = -(value * flag)
            column_ref[node, k] = value
            high, low = split(value)
            left_high, left_low = panel_high[node, b], panel_low[node, b]
            term = tdot(left_high, high) + tdot(left_high, low) + tdot(left_low, high)
            total = term if total is None else total + term
        cross[pl.ds(node * width, width), :] = total
        return carry

    lax.fori_loop(0, nodes, close, 0)

    share = nodes * width // grid_cols

    def piece(index):
        return pl.ds(pl.multiple_of(index * share, 8), share)

    def one(j):
        target = lax.rem(col + j, grid_cols)
        return pltpu.make_async_remote_copy(
            src_ref=cross.at[piece(target)], dst_ref=slices.at[j],
            send_sem=one_send.at[j], recv_sem=one_recv.at[j],
            device_id=(row, target), device_id_type=MESH,
        )

    def two(j):
        target = lax.rem(row + j, grid_rows)
        return pltpu.make_async_remote_copy(
            src_ref=sums.at[row], dst_ref=sums.at[row],
            send_sem=two_send.at[j], recv_sem=two_recv.at[j],
            device_id=(target, col), device_id_type=MESH,
        )

    def two_arrival(j):
        source = lax.rem(row - j + grid_rows, grid_rows)
        return pltpu.make_async_remote_copy(
            src_ref=sums.at[source], dst_ref=sums.at[source],
            send_sem=two_send.at[j], recv_sem=two_recv.at[j],
            device_id=(source, col), device_id_type=MESH,
        )

    def three(j):
        target = lax.rem(col + j, grid_cols)
        return pltpu.make_async_remote_copy(
            src_ref=whole.at[piece(col)], dst_ref=whole.at[piece(col)],
            send_sem=three_send.at[j], recv_sem=three_recv.at[j],
            device_id=(row, target), device_id_type=MESH,
        )

    def three_arrival(j):
        source = lax.rem(col - j + grid_cols, grid_cols)
        return pltpu.make_async_remote_copy(
            src_ref=whole.at[piece(source)], dst_ref=whole.at[piece(source)],
            send_sem=three_send.at[j], recv_sem=three_recv.at[j],
            device_id=(row, source), device_id_type=MESH,
        )

    def each(count, action):
        def body(j, carry):
            action(j)
            return carry

        lax.fori_loop(1, count, body, 0)

    each(grid_cols, lambda j: one(j).start())
    each(grid_cols, lambda j: one(j).wait_recv())
    value = cross[piece(col), :]
    for j in range(1, grid_cols):
        value = value + slices[j]
    sums[row] = value
    each(grid_rows, lambda j: two(j).start())
    each(grid_rows, lambda j: two_arrival(j).wait_recv())
    value = sums[0]
    for j in range(1, grid_rows):
        value = value + sums[j]
    whole[piece(col), :] = diag_ref[piece(col), :] - value
    each(grid_cols, lambda j: three(j).start())
    each(grid_cols, lambda j: three_arrival(j).wait_recv())
    out_ref[...] = whole[...]
    each(grid_cols, lambda j: one(j).wait_send())
    each(grid_rows, lambda j: two(j).wait_send())
    each(grid_cols, lambda j: three(j).wait_send())

    def leave(d, carry):
        copy, mine, _ = send_copy(d)

        @pl.when(jnp.logical_not(mine))
        def _():
            copy.wait_send()

        return carry

    lax.fori_loop(0, col_blocks, leave, 0)

    def leave_hop(slot, carry):
        target = lax.rem(slot, grid_rows)

        @pl.when(row < target)
        def _():
            hop(slot, 0, row + 1).wait_send()

        @pl.when(row > target)
        def _():
            hop(slot, 1, row - 1).wait_send()

        return carry

    lax.fori_loop(0, slots, leave_hop, 0)


def local(ancestor_inverse, panel, pattern, diag_term):
    grid_rows = lax.axis_size("prow")
    grid_cols = lax.axis_size("pcol")
    nodes, row_blocks, _, block, width = panel.shape
    col_blocks = ancestor_inverse.shape[3]
    kept = row_blocks // grid_cols
    f32 = jnp.float32
    share = nodes * width // grid_cols
    dma = pltpu.SemaphoreType.DMA
    vmem = pl.BlockSpec(memory_space=pltpu.VMEM)
    column, diag = pl.pallas_call(
        functools.partial(kernel, grid_rows, grid_cols),
        out_shape=(
            jax.ShapeDtypeStruct((nodes, kept, block, width), f32),
            jax.ShapeDtypeStruct((nodes * width, width), f32),
        ),
        in_specs=[
            pl.BlockSpec(memory_space=pl.ANY),
            vmem,
            pl.BlockSpec(memory_space=pltpu.SMEM),
            vmem,
        ],
        out_specs=(vmem, vmem),
        scratch_shapes=[
            pltpu.VMEM((nodes, row_blocks, block, width), jnp.bfloat16),
            pltpu.VMEM((nodes, row_blocks, block, width), jnp.bfloat16),
            pltpu.VMEM((2, row_blocks, block, block), f32),
            pltpu.VMEM((col_blocks, nodes, block, width), f32),
            pltpu.VMEM((kept * grid_rows, nodes, block, width), f32),
            pltpu.VMEM((2 * kept * grid_rows, nodes, block, width), f32),
            pltpu.VMEM((nodes * width, width), f32),
            pltpu.VMEM((grid_cols, share, width), f32),
            pltpu.VMEM((grid_rows, share, width), f32),
            pltpu.VMEM((nodes * width, width), f32),
            dma((2,)),
            dma((col_blocks,)),
            dma((kept * grid_rows,)),
            dma((kept * grid_rows,)),
            dma((2 * kept * grid_rows,)),
            dma((grid_cols,)),
            dma((grid_cols,)),
            dma((grid_rows,)),
            dma((grid_rows,)),
            dma((grid_cols,)),
            dma((grid_cols,)),
        ],
        compiler_params=pltpu.CompilerParams(
            has_side_effects=True, vmem_limit_bytes=52 * 1024 * 1024
        ),
    )(
        ancestor_inverse,
        panel.reshape(nodes, row_blocks, block, width),
        pattern,
        diag_term.reshape(nodes * width, width),
    )
    return column[:, :, None], diag.reshape(nodes, width, width)


def solution(mesh):
    in_specs = (
        P(None, "prow", None, None, "pcol", None),
        P(None, None, "prow", None, None),
        P(),
        P(),
    )
    out_specs = (P(None, "pcol", "prow", None, None), P())
    return jax.shard_map(local, mesh=mesh, in_specs=in_specs, out_specs=out_specs, check_vma=False)
```
